32 devices in a mesh: dp: 16 (over z, y, x), cuts: 2 (over core).
Axes of the slice: x: 2, y: 2, z: 4, core: 2. Of those that a mesh axis runs over, the one named last changes fastest.
Arguments:
- activations: bfloat16 [12288, 8192], P('dp', 'cuts'), may hold values from -6 to 6
- out_grads: bfloat16 [12288, 512], P('dp'), may hold values from -0.16210938 to 0.16210938
- weight: bfloat16 [512, 8192], P('dp', 'cuts'), may hold values from -0.0625 to 0.0625
- left_basis: bfloat16 [16, 512, 512], P('cuts'), may hold values from -0.25 to 0.25
- right_basis: bfloat16 [16, 512, 512], P('cuts'), may hold values from -0.25 to 0.25
- first_moment: float32 [512, 16, 512], P('dp', 'cuts'), may hold values from -3 to 3
- second_moment: float32 [512, 16, 512], P('dp', 'cuts'), may hold values from 0.05 to 2
Outputs:
- layer_output: bfloat16 [12288, 512], P('dp', 'cuts')
- new_weight: bfloat16 [512, 8192], P('dp', 'cuts')
- new_first: float32 [512, 16, 512], P('dp', 'cuts')
- new_second: float32 [512, 16, 512], P('dp', 'cuts')
The draws below stay inside these ranges and needn't reach their ends.
All inputs are finite; a program needn't handle non-finite values.
Results may differ from the reference program's by a relative error of at most 0.0048.
Values may be sent and summed in bfloat16 or wider, within the bound.
A program may use at most 128 MiB of HBM per device.

```python
import math
import jax
import jax.numpy as jnp
from jax import lax

D = 8192
KV = 512
BLK = 512
STEP = 10
TOK_DEV = 768
TOKENS = 12288
NB = 16
N_DP = 16


def raised(values, key, source, target, blocks, factor):
    def block_of(position):
        return (jnp.arange(values.shape[position]) // (values.shape[position] // blocks)).reshape((-1,) + (1,) * (values.ndim - 1 - position))

    near = jax.random.permutation(key, blocks)[block_of(target)]
    second = (block_of(target) + blocks // 2) % blocks
    return jnp.where((block_of(source) == near) | (block_of(source) == second), factor * values, values)


def shard_levels(key, dims, shards, smallest, top_value):
    def one(dim, shards_of):
        heights = jax.random.uniform(jax.random.fold_in(jax.random.fold_in(key, 6), dim), (shards_of,), jnp.float32, smallest / len(shards), top_value / len(shards))
        return jnp.repeat(jnp.exp(heights), dims[dim] // shards_of).reshape((-1,) + (1,) * (len(dims) - dim - 1))

    loudness = one(*shards[0])
    for cut in shards[1:]:
        loudness = loudness * one(*cut)
    return loudness


def noise(key, extent, spread, reach, shards=(), dtype=jnp.bfloat16):
    result = spread * jax.random.normal(key, extent, jnp.float32)
    if shards:
        result = result * shard_levels(key, extent, shards, -0.22, 0.18)
    return jnp.clip(result, -reach, reach).astype(dtype)


def gaussian_with(rng, shape, deviation, limit, split, heavy, dtype=jnp.bfloat16):
    result = deviation * jax.random.normal(rng, shape, jnp.float32)
    if split:
        result = result * shard_levels(rng, shape, split, -0.22, 0.18)
    return jnp.clip(raised(result, jax.random.fold_in(rng, 3), *heavy), -limit, limit).astype(dtype)


def setup_inputs(seed: int = 0) -> dict:
    key_list = jax.random.split(jax.random.key(seed), 8)
    return {
        "activations": noise(key_list[0], (TOKENS, D), 1.0, 6.0, ((0, 16), (1, 2))),
        "out_grads": gaussian_with(key_list[1], (TOKENS, KV), (3.0 / (TOK_DEV * N_DP) ** 0.5), 0.16210938, ((0, 16),), (0, 1, 16, 2.0)),
        "weight": noise(key_list[2], (KV, D), D ** -0.5, 0.0625, ((0, 16), (1, 2))),
        "left_basis": noise(key_list[3], (NB, BLK, BLK), BLK ** -0.5, 0.25, ((0, 2),)),
        "right_basis": noise(key_list[4], (NB, KV, KV), KV ** -0.5, 0.25, ((0, 2),)),
        "first_moment": noise(key_list[5], (BLK, NB, KV), 0.5, 3.0, ((0, 16), (1, 2)), jnp.float32),
        "second_moment": jnp.clip(jnp.exp(math.log(2.0) - 3.6888794 * jax.random.uniform(key_list[6], (BLK, NB, KV), jnp.float32) ** shard_levels(key_list[6], (BLK, NB, KV), ((0, 16), (1, 2)), -0.2, 0.2)), 0.05, 2.0),
    }


LEARNING_RATE = 0.02
epsilon = 1e-08

def reference(activations, out_grads, weight, left_basis, right_basis, first_moment, second_moment):
    highest = lax.Precision.HIGHEST
    grads = lax.dot_general(out_grads, activations, (((0,), (0,)), ((), ())), preferred_element_type=jnp.float32)
    grads = grads.reshape(KV, NB, BLK)
    left_full = left_basis.astype(jnp.float32)
    right_full = right_basis.astype(jnp.float32)
    left_turned = jnp.einsum('cgr,grk->kgc', grads, left_full, precision=highest)
    rotated = jnp.einsum('kgc,gcd->kgd', left_turned, right_full, precision=highest)
    new_first = 0.9 * first_moment + 0.1 * rotated
    new_second = 0.95 * second_moment + 0.05 * rotated * rotated
    bias_first = 1.0 - 0.9 ** STEP
    bias_second = 1.0 - 0.95 ** STEP
    direction = new_first / bias_first / (jnp.sqrt(new_second / bias_second) + epsilon)
    back_turned = jnp.einsum('kgd,gcd->kgc', direction, right_full, precision=highest)
    update = jnp.einsum('kgc,grk->cgr', back_turned, left_full, precision=highest).reshape(KV, D)
    new_weight = (weight.astype(jnp.float32) - LEARNING_RATE * update).astype(jnp.bfloat16)
    layer_output = lax.dot_general(activations, new_weight, (((1,), (1,)), ((), ())), preferred_element_type=jnp.float32)
    return (layer_output.astype(jnp.bfloat16), new_weight, new_first, new_second)
```

```python
import jax
import jax.numpy as jnp
from jax import lax
from jax.experimental import pallas as pl
from jax.experimental.pallas import tpu as pltpu
from jax.sharding import PartitionSpec as P

STEP = 10


LEARNING_RATE = 0.02
epsilon = 1e-08
MESH = pl.DeviceIdType.MESH
BF = jnp.bfloat16
F32 = jnp.float32


def local(activations, out_grads, weight, left_basis, right_basis, first_moment, second_moment):
    highest = lax.Precision.HIGHEST
    left_full = left_basis.astype(jnp.float32)
    right_full = right_basis.astype(jnp.float32)
    num_blocks = left_full.shape[0]
    block_rows = left_full.shape[1]
    grad_slab = lax.psum_scatter(
        lax.dot_general(
            out_grads, activations, (((0,), (0,)), ((), ())), preferred_element_type=jnp.float32
        ),
        "dp",
        scatter_dimension=0,
        tiled=True,
    )
    grad_slab = grad_slab.reshape(grad_slab.shape[0], num_blocks, block_rows)
    left_turned = jnp.einsum("cbr,brk->cbk", grad_slab, left_full, precision=highest)
    regrouped = lax.all_to_all(left_turned, "dp", split_axis=2, concat_axis=0, tiled=True)
    rotated = jnp.einsum("cbk,bcd->kbd", regrouped, right_full, precision=highest)
    new_first = 0.9 * first_moment + 0.1 * rotated
    new_second = 0.95 * second_moment + 0.05 * rotated * rotated
    bias_first = 1.0 - 0.9**STEP
    bias_second = 1.0 - 0.95**STEP
    direction = new_first / bias_first / (jnp.sqrt(new_second / bias_second) + epsilon)
    back_turned = jnp.einsum("kbd,bcd->kbc", direction, right_full, precision=highest)
    returned = lax.all_to_all(back_turned, "dp", split_axis=2, concat_axis=0, tiled=True)
    update = jnp.einsum("kbc,brk->cbr", returned, left_full, precision=highest).reshape(
        weight.shape
    )
    new_weight = (weight.astype(jnp.float32) - LEARNING_RATE * update).astype(jnp.bfloat16)
    partial_out = lax.dot_general(
        activations,
        lax.all_gather(new_weight, "dp", axis=0, tiled=True),
        (((1,), (1,)), ((), ())),
        preferred_element_type=jnp.float32,
    )
    layer_output = lax.psum_scatter(partial_out, "cuts", scatter_dimension=1, tiled=True).astype(
        jnp.bfloat16
    )
    return (layer_output, new_weight, new_first, new_second)


def split_dot(values, basis, dims):
    high = values.astype(BF)
    low = (values - high.astype(F32)).astype(BF)
    return lax.dot_general(high, basis, dims, preferred_element_type=F32) + lax.dot_general(
        low, basis, dims, preferred_element_type=F32
    )


ROWS_COLS = (((1,), (0,)), ((), ()))
ROWS_ROWS = (((1,), (1,)), ((), ()))


def kernel(
    act_h, og_h, w_h, left_h, right_h, m_h, v_h,
    out_h, nw_h, nf_h, ns_h,
    act, og, w, left, right, m, v, turned,
    s1, r1, keep1, s2, r2, keep2, zs, zr, slab,
    a_send, a_recv, b_send, b_recv, flip, nf, ns,
    full, po, po_recv, out,
    load_sem, act_sem, store_sem,
    s1_sem, r1_sem, s2_sem, r2_sem, zs_sem, zr_sem,
    as_sem, ar_sem, bs_sem, br_sem,
    gz_s, gz_r, gx_s, gx_r, gy_s, gy_r, gf_s, gf_r, c_s, c_r,
):
    me = lax.axis_index("dp")
    core = lax.axis_index("cuts")
    z, plane = me // 4, me % 4
    bits = (me % 2, (me // 2) % 2)
    n = 16
    nb = 8
    near = (me + 1 - 2 * bits[0], me + 2 - 4 * bits[1])

    def remote(src, dst, ss, rs, target):
        return pltpu.make_async_remote_copy(
            src_ref=src, dst_ref=dst, send_sem=ss, recv_sem=rs,
            device_id=(target, core), device_id_type=MESH,
        )

    acts = [
        pltpu.make_async_copy(
            act_h.at[:, pl.ds(i * 512, 512)], act.at[:, pl.ds(i * 512, 512)], act_sem.at[i]
        )
        for i in range(nb)
    ]
    loads = [
        pltpu.make_async_copy(a, b, load_sem.at[i])
        for i, (a, b) in enumerate(
            ((og_h, og), (left_h, left), (right_h, right), (m_h, m), (v_h, v), (w_h, w))
        )
    ]
    loads[0].start()
    for c in acts + loads[1:]:
        c.start()

    barrier = pltpu.get_barrier_semaphore()
    for j in range(1, n):
        pl.semaphore_signal(
            barrier, inc=1, device_id=(lax.rem(me + j, n), core), device_id_type=MESH
        )
    pl.semaphore_signal(barrier, inc=1, device_id=(me, 1 - core), device_id_type=MESH)

    loads[0].wait()
    across = og[...].T
    for zz in range(4):
        for yy in range(2):
            for xx in range(2):
                at = zz * 128 + yy * 64 + xx * 32
                piece = across[at : at + 32]
                turned[0, xx, pl.ds(yy * 128 + zz * 32, 32)] = piece
                turned[1, yy, pl.ds(xx * 128 + zz * 32, 32)] = piece
    pl.semaphore_wait(barrier, n)

    pending = []

    first = []
    for i in range(nb):
        h = i % 2
        acts[i].wait()
        block = act[:, i * 512 : (i + 1) * 512]
        s1[i] = (
            lax.dot_general(turned[h, 1 - bits[h]], block, ROWS_COLS, preferred_element_type=F32)
            .astype(BF)
            .reshape(2, 128, 512)
        )
        copy = remote(s1.at[i], r1.at[i], s1_sem.at[i], r1_sem.at[i], near[h])
        copy.start()
        first.append(copy)
        keep1[i] = lax.dot_general(
            turned[h, bits[h]], block, ROWS_COLS, preferred_element_type=F32
        ).reshape(2, 128, 512)
    pending += first

    second = []

    def stage2(i):
        h = i % 2
        b = bits[1 - h]
        first[i].wait_recv()
        s2[i] = (keep1[i, 1 - b] + r1[i, 1 - b].astype(F32)).astype(BF).reshape(4, 32, 512)
        copy = remote(s2.at[i], r2.at[i], s2_sem.at[i], r2_sem.at[i], near[1 - h])
        copy.start()
        second.append(copy)
        pending.append(copy)
        keep2[i] = (keep1[i, b] + r1[i, b].astype(F32)).reshape(4, 32, 512)

    third = {}

    def stage3(i):
        second[i].wait_recv()
        for j in (2, 1, 3):
            to = lax.rem(z + j, 4)
            zs[i, j - 1] = (keep2[i, to] + r2[i, to].astype(F32)).astype(BF)
            copy = remote(
                zs.at[i, j - 1], zr.at[i, j - 1], zs_sem.at[i, j - 1], zr_sem.at[i, j - 1],
                to * 4 + plane,
            )
            copy.start()
            third[i, j] = copy
            pending.append(copy)

    def finish(i):
        total = keep2[i, z] + r2[i, z].astype(F32)
        for j in (1, 2, 3):
            third[i, j].wait_recv()
            total = total + zr[i, j - 1].astype(F32)
        if i == 0:
            loads[1].wait()
        slab[i] = split_dot(total, left[i], ROWS_COLS)

    def pack(buffer, group):
        blocks = [slab[4 * group + q] for q in range(4)]
        for d in range(n):
            buffer[group, d] = jnp.concatenate(
                [b[:, d * 32 : d * 32 + 32] for b in blocks], axis=1
            ).astype(BF)

    def send_all(buffer, landing, ss, rs, group):
        copies = []
        for j in range(1, n):
            to = lax.rem(me + j, n)
            copy = remote(
                buffer.at[group, to], landing.at[group, me], ss.at[group, j - 1],
                rs.at[group, j - 1], to,
            )
            copy.start()
            copies.append(copy)
        landing[group, me] = buffer[group, me]
        pending.extend(copies)
        return copies

    a_copies = {}
    for t in range(nb + 4):
        if t < nb:
            stage2(t)
        if 0 <= t - 2 < nb:
            stage3(t - 2)
        if 0 <= t - 4 < nb:
            finish(t - 4)
            if (t - 4) % 4 == 3:
                group = (t - 4) // 4
                pack(a_send, group)
                a_copies[group] = send_all(a_send, a_recv, as_sem, ar_sem, group)

    for c in loads[2:]:
        c.wait()

    bias_first = 1.0 - 0.9**STEP
    bias_second = 1.0 - 0.95**STEP
    b_copies = {}
    for group in range(2):
        for c in a_copies[group]:
            c.wait_recv()
        flip[...] = a_recv[group].reshape(512, 128).T
        for q in range(4):
            g = 4 * group + q
            rotated = lax.dot_general(
                flip[q * 32 : q * 32 + 32], right[g], ROWS_COLS, preferred_element_type=F32
            )
            new_first = 0.9 * m[:, g, :] + 0.1 * rotated
            new_second = 0.95 * v[:, g, :] + 0.05 * rotated * rotated
            nf[:, g, :] = new_first
            ns[:, g, :] = new_second
            direction = new_first / bias_first / (jnp.sqrt(new_second / bias_second) + epsilon)
            slab[g] = split_dot(direction, right[g], ROWS_ROWS)
        pack(b_send, group)
        b_copies[group] = send_all(b_send, b_recv, bs_sem, br_sem, group)

    stores = [
        pltpu.make_async_copy(nf, nf_h, store_sem.at[0]),
        pltpu.make_async_copy(ns, ns_h, store_sem.at[1]),
    ]
    for c in stores:
        c.start()

    def part(index, h):
        return full.at[index, :, pl.ds(h * 2048, 2048)]

    from_z, from_x, from_y, passed = {}, {}, {}, {}

    def spread(h, jj):
        index = lax.rem(z + 4 - jj, 4) * 4 + plane
        piece = part(index, h)
        from_x[h, jj] = remote(piece, piece, gx_s.at[h, jj], gx_r.at[h, jj], near[0])
        from_y[h, jj] = remote(piece, piece, gy_s.at[h, jj], gy_r.at[h, jj], near[1])
        from_x[h, jj].start()
        from_y[h, jj].start()
        pending.extend([from_x[h, jj], from_y[h, jj]])

    def forward(h, jj):
        row = lax.rem(z + 4 - jj, 4) * 4
        if h == 0:
            from_y[h, jj].wait_recv()
            piece = part(row + (near[1] % 4), h)
            target = near[0]
        else:
            from_x[h, jj].wait_recv()
            piece = part(row + (near[0] % 4), h)
            target = near[1]
        passed[h, jj] = remote(piece, piece, gf_s.at[h, jj], gf_r.at[h, jj], target)
        passed[h, jj].start()
        pending.append(passed[h, jj])

    for h in range(2):
        for c in b_copies[h]:
            c.wait_recv()
        flip[...] = b_recv[h].reshape(512, 128).T
        for q in range(4):
            g = 4 * h + q
            update = lax.dot_general(
                flip[q * 32 : q * 32 + 32], left[g], ROWS_ROWS, preferred_element_type=F32
            )
            columns = slice(g * 512, (g + 1) * 512)
            full[me, :, columns] = (
                w[:, columns].astype(F32) - LEARNING_RATE * update
            ).astype(BF)
        for jj in (2, 1, 3):
            piece = part(me, h)
            from_z[h, jj] = remote(
                piece, piece, gz_s.at[h, jj - 1], gz_r.at[h, jj - 1], lax.rem(z + jj, 4) * 4 + plane
            )
            from_z[h, jj].start()
            pending.append(from_z[h, jj])
        spread(h, 0)

    stores.append(pltpu.make_async_copy(full.at[me], nw_h, store_sem.at[2]))
    stores[2].start()

    def product(jj):
        row = lax.rem(z + 4 - jj, 4)
        for h in range(2):
            (from_x if h == 0 else from_y)[h, jj].wait_recv()
            passed[h, jj].wait_recv()
        po[row] = lax.dot_general(
            act[...], full[pl.ds(row * 4, 4)].reshape(128, 4096), ROWS_ROWS,
            preferred_element_type=F32,
        )

    order = (0, 1, 3, 2)
    for a, jj in enumerate(order):
        for h in range(2):
            if jj:
                from_z[h, jj].wait_recv()
                spread(h, jj)
            if a:
                forward(h, order[a - 1])
        if a > 1:
            product(order[a - 2])
    for h in range(2):
        forward(h, order[3])
    product(order[2])
    product(order[3])

    swap = pltpu.make_async_remote_copy(
        src_ref=po.at[pl.ds(2 - 2 * core, 2)], dst_ref=po_recv, send_sem=c_s, recv_sem=c_r,
        device_id=(me, 1 - core), device_id_type=MESH,
    )
    swap.start()
    for c in pending:
        c.wait_send()
    swap.wait_recv()
    for k in range(2):
        out[:, k * 128 : (k + 1) * 128] = (po[2 * core + k] + po_recv[k]).astype(BF)
    stores.append(pltpu.make_async_copy(out, out_h, store_sem.at[3]))
    stores[3].start()
    swap.wait_send()
    for c in stores:
        c.wait()


def fused(activations, out_grads, weight, left_basis, right_basis, first_moment, second_moment):
    any_space = pl.BlockSpec(memory_space=pl.ANY)
    dma = pltpu.SemaphoreType.DMA
    vm = pltpu.VMEM
    return pl.pallas_call(
        kernel,
        out_shape=(
            jax.ShapeDtypeStruct((768, 256), BF),
            jax.ShapeDtypeStruct((32, 4096), BF),
            jax.ShapeDtypeStruct((32, 8, 512), F32),
            jax.ShapeDtypeStruct((32, 8, 512), F32),
        ),
        in_specs=[any_space] * 7,
        out_specs=(any_space,) * 4,
        scratch_shapes=[
            vm((768, 4096), BF), vm((768, 512), BF), vm((32, 4096), BF),
            vm((8, 512, 512), BF), vm((8, 512, 512), BF),
            vm((32, 8, 512), F32), vm((32, 8, 512), F32), vm((2, 2, 256, 768), BF),
            vm((8, 2, 128, 512), BF), vm((8, 2, 128, 512), BF), vm((8, 2, 128, 512), F32),
            vm((8, 4, 32, 512), BF), vm((8, 4, 32, 512), BF), vm((8, 4, 32, 512), F32),
            vm((8, 3, 32, 512), BF), vm((8, 3, 32, 512), BF), vm((8, 32, 512), F32),
            vm((2, 16, 32, 128), BF), vm((2, 16, 32, 128), BF),
            vm((2, 16, 32, 128), BF), vm((2, 16, 32, 128), BF),
            vm((128, 512), BF), vm((32, 8, 512), F32), vm((32, 8, 512), F32),
            vm((16, 32, 4096), BF), vm((4, 768, 128), F32), vm((2, 768, 128), F32),
            vm((768, 256), BF),
            dma((6,)), dma((8,)), dma((4,)),
            dma((8,)), dma((8,)), dma((8,)), dma((8,)), dma((8, 3)), dma((8, 3)),
            dma((2, 15)), dma((2, 15)), dma((2, 15)), dma((2, 15)),
            dma((2, 3)), dma((2, 3)), dma((2, 4)), dma((2, 4)), dma((2, 4)), dma((2, 4)),
            dma((2, 4)), dma((2, 4)), dma, dma,
        ],
        compiler_params=pltpu.CompilerParams(
            collective_id=0, has_side_effects=True, vmem_limit_bytes=60 * 1024 * 1024
        ),
    )(activations, out_grads, weight, left_basis, right_basis, first_moment, second_moment)


def solution(mesh):
    placed = (
        P("dp", "cuts"),
        P("dp", None),
        P("dp", "cuts"),
        P("cuts", None, None),
        P("cuts", None, None),
        P("dp", "cuts", None),
        P("dp", "cuts", None),
    )
    small = mesh.shape["dp"] == 16 and mesh.shape["cuts"] == 2
    return jax.shard_map(
        fused if small else local,
        mesh=mesh,
        in_specs=placed,
        out_specs=(P("dp", "cuts"), P("dp", "cuts"), P("dp", "cuts", None), P("dp", "cuts", None)),
        check_vma=False,
    )
```

```python
import jax
import jax.numpy as jnp
from jax import lax
from jax.experimental import pallas as pl
from jax.experimental.pallas import tpu as pltpu
from jax.sharding import PartitionSpec as P

STEP = 10


LEARNING_RATE = 0.02
epsilon = 1e-08
MESH = pl.DeviceIdType.MESH
BF = jnp.bfloat16
F32 = jnp.float32


def local(activations, out_grads, weight, left_basis, right_basis, first_moment, second_moment):
    highest = lax.Precision.HIGHEST
    left_full = left_basis.astype(jnp.float32)
    right_full = right_basis.astype(jnp.float32)
    num_blocks = left_full.shape[0]
    block_rows = left_full.shape[1]
    grad_slab = lax.psum_scatter(
        lax.dot_general(
            out_grads, activations, (((0,), (0,)), ((), ())), preferred_element_type=jnp.float32
        ),
        "dp",
        scatter_dimension=0,
        tiled=True,
    )
    grad_slab = grad_slab.reshape(grad_slab.shape[0], num_blocks, block_rows)
    left_turned = jnp.einsum("cbr,brk->cbk", grad_slab, left_full, precision=highest)
    regrouped = lax.all_to_all(left_turned, "dp", split_axis=2, concat_axis=0, tiled=True)
    rotated = jnp.einsum("cbk,bcd->kbd", regrouped, right_full, precision=highest)
    new_first = 0.9 * first_moment + 0.1 * rotated
    new_second = 0.95 * second_moment + 0.05 * rotated * rotated
    bias_first = 1.0 - 0.9**STEP
    bias_second = 1.0 - 0.95**STEP
    direction = new_first / bias_first / (jnp.sqrt(new_second / bias_second) + epsilon)
    back_turned = jnp.einsum("kbd,bcd->kbc", direction, right_full, precision=highest)
    returned = lax.all_to_all(back_turned, "dp", split_axis=2, concat_axis=0, tiled=True)
    update = jnp.einsum("kbc,brk->cbr", returned, left_full, precision=highest).reshape(
        weight.shape
    )
    new_weight = (weight.astype(jnp.float32) - LEARNING_RATE * update).astype(jnp.bfloat16)
    partial_out = lax.dot_general(
        activations,
        lax.all_gather(new_weight, "dp", axis=0, tiled=True),
        (((1,), (1,)), ((), ())),
        preferred_element_type=jnp.float32,
    )
    layer_output = lax.psum_scatter(partial_out, "cuts", scatter_dimension=1, tiled=True).astype(
        jnp.bfloat16
    )
    return (layer_output, new_weight, new_first, new_second)


def split_dot(values, basis, dims):
    high = values.astype(BF)
    low = (values - high.astype(F32)).astype(BF)
    return lax.dot_general(high, basis, dims, preferred_element_type=F32) + lax.dot_general(
        low, basis, dims, preferred_element_type=F32
    )


ROWS_COLS = (((1,), (0,)), ((), ()))
ROWS_ROWS = (((1,), (1,)), ((), ()))


def kernel(
    act_h, og_h, w_h, left_h, right_h, m_h, v_h,
    out_h, nw_h, nf_h, ns_h,
    act, og, w, left, right, m, v, turned,
    s1, r1, keep1, s2, r2, keep2, zs, zr, slab,
    a_send, a_recv, b_send, b_recv, flip, nf, ns,
    full, po, po_recv, out,
    load_sem, act_sem, store_sem,
    s1_sem, r1_sem, s2_sem, r2_sem, zs_sem, zr_sem,
    as_sem, ar_sem, bs_sem, br_sem,
    gz_s, gz_r, gx_s, gx_r, gy_s, gy_r, gf_s, gf_r, c_s, c_r,
):
    me = lax.axis_index("dp")
    core = lax.axis_index("cuts")
    z, plane = me // 4, me % 4
    bits = (me % 2, (me // 2) % 2)
    n = 16
    nb = 8
    near = (me + 1 - 2 * bits[0], me + 2 - 4 * bits[1])

    def remote(src, dst, ss, rs, target):
        return pltpu.make_async_remote_copy(
            src_ref=src, dst_ref=dst, send_sem=ss, recv_sem=rs,
            device_id=(target, core), device_id_type=MESH,
        )

    acts = [
        pltpu.make_async_copy(
            act_h.at[:, pl.ds(i * 512, 512)], act.at[:, pl.ds(i * 512, 512)], act_sem.at[i]
        )
        for i in range(nb)
    ]
    loads = [
        pltpu.make_async_copy(a, b, load_sem.at[i])
        for i, (a, b) in enumerate(
            ((og_h, og), (left_h, left), (right_h, right), (m_h, m), (v_h, v), (w_h, w))
        )
    ]
    loads[0].start()
    for c in acts + loads[1:]:
        c.start()

    barrier = pltpu.get_barrier_semaphore()
    for j in range(1, n):
        pl.semaphore_signal(
            barrier, inc=1, device_id=(lax.rem(me + j, n), core), device_id_type=MESH
        )
    pl.semaphore_signal(barrier, inc=1, device_id=(me, 1 - core), device_id_type=MESH)

    loads[0].wait()
    across = og[...].T
    for zz in range(4):
        for yy in range(2):
            for xx in range(2):
                at = zz * 128 + yy * 64 + xx * 32
                piece = across[at : at + 32]
                turned[0, xx, pl.ds(yy * 128 + zz * 32, 32)] = piece
                turned[1, yy, pl.ds(xx * 128 + zz * 32, 32)] = piece

    pending = []

    first = []
    for i in range(nb):
        h = i % 2
        acts[i].wait()
        block = act[:, i * 512 : (i + 1) * 512]
        s1[i] = (
            lax.dot_general(turned[h, 1 - bits[h]], block, ROWS_COLS, preferred_element_type=F32)
            .astype(BF)
            .reshape(2, 128, 512)
        )
        first.append(remote(s1.at[i], r1.at[i], s1_sem.at[i], r1_sem.at[i], near[h]))
        if i == 0:
            pl.semaphore_wait(barrier, n)
        if i < 4:
            first[i].start()
        keep1[i] = lax.dot_general(
            turned[h, bits[h]], block, ROWS_COLS, preferred_element_type=F32
        ).reshape(2, 128, 512)
    pending += first

    def first_start(i):
        first[i].start()

    second = []

    def stage2(i):
        h = i % 2
        b = bits[1 - h]
        first[i].wait_recv()
        s2[i] = (keep1[i, 1 - b] + r1[i, 1 - b].astype(F32)).astype(BF).reshape(4, 32, 512)
        copy = remote(s2.at[i], r2.at[i], s2_sem.at[i], r2_sem.at[i], near[1 - h])
        copy.start()
        second.append(copy)
        pending.append(copy)
        keep2[i] = (keep1[i, b] + r1[i, b].astype(F32)).reshape(4, 32, 512)

    third = {}

    def stage3(i):
        second[i].wait_recv()
        for j in (2, 1, 3):
            to = lax.rem(z + j, 4)
            zs[i, j - 1] = (keep2[i, to] + r2[i, to].astype(F32)).astype(BF)
            copy = remote(
                zs.at[i, j - 1], zr.at[i, j - 1], zs_sem.at[i, j - 1], zr_sem.at[i, j - 1],
                to * 4 + plane,
            )
            copy.start()
            third[i, j] = copy
            pending.append(copy)

    def finish(i):
        total = keep2[i, z] + r2[i, z].astype(F32)
        for j in (1, 2, 3):
            third[i, j].wait_recv()
            total = total + zr[i, j - 1].astype(F32)
        if i == 0:
            loads[1].wait()
        slab[i] = split_dot(total, left[i], ROWS_COLS)

    def pack(buffer, group):
        blocks = [slab[4 * group + q] for q in range(4)]
        for d in range(n):
            buffer[group, d] = jnp.concatenate(
                [b[:, d * 32 : d * 32 + 32] for b in blocks], axis=1
            ).astype(BF)

    def send_all(buffer, landing, ss, rs, group):
        copies = []
        for j in range(1, n):
            to = lax.rem(me + j, n)
            copy = remote(
                buffer.at[group, to], landing.at[group, me], ss.at[group, j - 1],
                rs.at[group, j - 1], to,
            )
            copy.start()
            copies.append(copy)
        landing[group, me] = buffer[group, me]
        pending.extend(copies)
        return copies

    a_copies = {}

    def regroup(group):
        pack(a_send, group)
        a_copies[group] = send_all(a_send, a_recv, as_sem, ar_sem, group)

    for act_on, pair in (
        (stage2, 0), (first_start, 4), (stage2, 2), (first_start, 6), (stage3, 0), (stage2, 4),
        (stage3, 2), (finish, 0), (stage2, 6), (stage3, 4), (finish, 2),
    ):
        act_on(pair)
        act_on(pair + 1)
    regroup(0)
    for act_on, pair in ((stage3, 6), (finish, 4), (finish, 6)):
        act_on(pair)
        act_on(pair + 1)
    regroup(1)

    for c in loads[2:]:
        c.wait()

    bias_first = 1.0 - 0.9**STEP
    bias_second = 1.0 - 0.95**STEP
    b_copies = {}
    for group in range(2):
        for c in a_copies[group]:
            c.wait_recv()
        flip[...] = a_recv[group].reshape(512, 128).T
        for q in range(4):
            g = 4 * group + q
            rotated = lax.dot_general(
                flip[q * 32 : q * 32 + 32], right[g], ROWS_COLS, preferred_element_type=F32
            )
            new_first = 0.9 * m[:, g, :] + 0.1 * rotated
            new_second = 0.95 * v[:, g, :] + 0.05 * rotated * rotated
            nf[:, g, :] = new_first
            ns[:, g, :] = new_second
            direction = new_first / bias_first / (jnp.sqrt(new_second / bias_second) + epsilon)
            slab[g] = split_dot(direction, right[g], ROWS_ROWS)
        pack(b_send, group)
        b_copies[group] = send_all(b_send, b_recv, bs_sem, br_sem, group)

    stores = [
        pltpu.make_async_copy(nf, nf_h, store_sem.at[0]),
        pltpu.make_async_copy(ns, ns_h, store_sem.at[1]),
    ]
    for c in stores:
        c.start()

    def part(index, h):
        return full.at[index, :, pl.ds(h * 2048, 2048)]

    meets = (z, z + 1 - 2 * (z % 2), lax.rem(z + 2, 4), 3 - z)
    from_z, from_x, from_y, passed = {}, {}, {}, {}

    def spread(h, jj):
        index = meets[jj] * 4 + plane
        piece = part(index, h)
        from_x[h, jj] = remote(piece, piece, gx_s.at[h, jj], gx_r.at[h, jj], near[0])
        from_y[h, jj] = remote(piece, piece, gy_s.at[h, jj], gy_r.at[h, jj], near[1])
        from_x[h, jj].start()
        from_y[h, jj].start()
        pending.extend([from_x[h, jj], from_y[h, jj]])

    def forward(h, jj):
        row = meets[jj] * 4
        if h == 0:
            from_y[h, jj].wait_recv()
            piece = part(row + (near[1] % 4), h)
            target = near[0]
        else:
            from_x[h, jj].wait_recv()
            piece = part(row + (near[0] % 4), h)
            target = near[1]
        passed[h, jj] = remote(piece, piece, gf_s.at[h, jj], gf_r.at[h, jj], target)
        passed[h, jj].start()
        pending.append(passed[h, jj])

    for h in range(2):
        for c in b_copies[h]:
            c.wait_recv()
        flip[...] = b_recv[h].reshape(512, 128).T
        for q in range(4):
            g = 4 * h + q
            update = lax.dot_general(
                flip[q * 32 : q * 32 + 32], left[g], ROWS_ROWS, preferred_element_type=F32
            )
            columns = slice(g * 512, (g + 1) * 512)
            full[me, :, columns] = (
                w[:, columns].astype(F32) - LEARNING_RATE * update
            ).astype(BF)
        spread(h, 0)
        for jj in (1, 2, 3):
            piece = part(me, h)
            from_z[h, jj] = remote(
                piece, piece, gz_s.at[h, jj - 1], gz_r.at[h, jj - 1], meets[jj] * 4 + plane
            )
            from_z[h, jj].start()
            pending.append(from_z[h, jj])

    stores.append(pltpu.make_async_copy(full.at[me], nw_h, store_sem.at[2]))
    stores[2].start()

    def product(jj):
        row = meets[jj]
        halves = []
        for h in range(2):
            (from_x if h == 0 else from_y)[h, jj].wait_recv()
            passed[h, jj].wait_recv()
            halves.append(
                lax.dot_general(
                    act[:, h * 2048 : (h + 1) * 2048],
                    full[pl.ds(row * 4, 4), :, h * 2048 : (h + 1) * 2048].reshape(128, 2048),
                    ROWS_ROWS,
                    preferred_element_type=F32,
                )
            )
        po[row] = halves[0] + halves[1]

    for jj in range(4):
        for h in range(2):
            if jj:
                from_z[h, jj].wait_recv()
                spread(h, jj)
        for h in range(2):
            forward(h, jj)
        if jj:
            product(jj - 1)
    product(3)

    swap = pltpu.make_async_remote_copy(
        src_ref=po.at[pl.ds(2 - 2 * core, 2)], dst_ref=po_recv, send_sem=c_s, recv_sem=c_r,
        device_id=(me, 1 - core), device_id_type=MESH,
    )
    swap.start()
    for c in pending:
        c.wait_send()
    swap.wait_recv()
    for k in range(2):
        out[:, k * 128 : (k + 1) * 128] = (po[2 * core + k] + po_recv[k]).astype(BF)
    stores.append(pltpu.make_async_copy(out, out_h, store_sem.at[3]))
    stores[3].start()
    swap.wait_send()
    for c in stores:
        c.wait()


def hand_over(*refs):
    for source, target in zip(refs[:4], refs[4:]):
        target[...] = source[...]


def fused(activations, out_grads, weight, left_basis, right_basis, first_moment, second_moment):
    any_space = pl.BlockSpec(memory_space=pl.ANY)
    dma = pltpu.SemaphoreType.DMA
    vm = pltpu.VMEM
    results = pl.pallas_call(
        kernel,
        out_shape=(
            jax.ShapeDtypeStruct((768, 256), BF),
            jax.ShapeDtypeStruct((32, 4096), BF),
            jax.ShapeDtypeStruct((32, 8, 512), F32),
            jax.ShapeDtypeStruct((32, 8, 512), F32),
        ),
        in_specs=[any_space] * 7,
        out_specs=(any_space,) * 4,
        scratch_shapes=[
            vm((768, 4096), BF), vm((768, 512), BF), vm((32, 4096), BF),
            vm((8, 512, 512), BF), vm((8, 512, 512), BF),
            vm((32, 8, 512), F32), vm((32, 8, 512), F32), vm((2, 2, 256, 768), BF),
            vm((8, 2, 128, 512), BF), vm((8, 2, 128, 512), BF), vm((8, 2, 128, 512), F32),
            vm((8, 4, 32, 512), BF), vm((8, 4, 32, 512), BF), vm((8, 4, 32, 512), F32),
            vm((8, 3, 32, 512), BF), vm((8, 3, 32, 512), BF), vm((8, 32, 512), F32),
            vm((2, 16, 32, 128), BF), vm((2, 16, 32, 128), BF),
            vm((2, 16, 32, 128), BF), vm((2, 16, 32, 128), BF),
            vm((128, 512), BF), vm((32, 8, 512), F32), vm((32, 8, 512), F32),
            vm((16, 32, 4096), BF), vm((4, 768, 128), F32), vm((2, 768, 128), F32),
            vm((768, 256), BF),
            dma((6,)), dma((8,)), dma((4,)),
            dma((8,)), dma((8,)), dma((8,)), dma((8,)), dma((8, 3)), dma((8, 3)),
            dma((2, 15)), dma((2, 15)), dma((2, 15)), dma((2, 15)),
            dma((2, 3)), dma((2, 3)), dma((2, 4)), dma((2, 4)), dma((2, 4)), dma((2, 4)),
            dma((2, 4)), dma((2, 4)), dma, dma,
        ],
        compiler_params=pltpu.CompilerParams(
            collective_id=0, has_side_effects=True, vmem_limit_bytes=60 * 1024 * 1024
        ),
    )(activations, out_grads, weight, left_basis, right_basis, first_moment, second_moment)


    return pl.pallas_call(
        hand_over,
        out_shape=tuple(jax.ShapeDtypeStruct(r.shape, r.dtype) for r in results),
    )(*results)


def solution(mesh):
    placed = (
        P("dp", "cuts"),
        P("dp", None),
        P("dp", "cuts"),
        P("cuts", None, None),
        P("cuts", None, None),
        P("dp", "cuts", None),
        P("dp", "cuts", None),
    )
    small = mesh.shape["dp"] == 16 and mesh.shape["cuts"] == 2
    return jax.shard_map(
        fused if small else local,
        mesh=mesh,
        in_specs=placed,
        out_specs=(P("dp", "cuts"), P("dp", "cuts"), P("dp", "cuts", None), P("dp", "cuts", None)),
        check_vma=False,
    )
```
